512 devices in a mesh: lat: 64 (over z, y), chan: 8 (over x, core).
Axes of the slice: x: 4, y: 8, z: 8, core: 2. Of those that a mesh axis runs over, the one named last changes fastest.
Arguments:
- field: float32 [256, 1105920], P('chan', 'lat'), may hold values from -6 to 6
- mixing: float32 [128, 2, 256, 256], P('lat', None, 'chan'), may hold values from -6 to 6
Outputs:
- result: float32 [256, 1105920], P('chan', 'lat')
The draws below stay inside these ranges and needn't reach their ends.
All inputs are finite; a program needn't handle non-finite values.
Results may differ from the reference program's by a relative error of at most 0.0003.
Values sent between devices are 32-bit elements; how exact they have to be, the bound alone decides.
A program may use at most 64 MiB of HBM per device.

```python
import jax
import jax.numpy as jnp
from jax import lax

C = 256
NLON = 1440
L = 121
MODES = 128
NLAT = 768


def block_scale(stream_key, dims, cuts, least, largest):
    level = 1.0
    for axis_at, blocks in cuts:
        steps = jax.random.uniform(jax.random.fold_in(jax.random.fold_in(stream_key, 6), axis_at), (blocks,), jnp.float32, least / len(cuts), largest / len(cuts))
        level = level * jnp.repeat(jnp.exp(steps), dims[axis_at] // blocks).reshape((-1,) + (1,) * (len(dims) - 1 - axis_at))
    return level


def gaussian(own_key, extent, deviation, limit, cuts=(), held_as=jnp.bfloat16):
    array = jax.random.normal(own_key, extent, jnp.float32) * deviation
    if len(cuts) > 0:
        array = block_scale(own_key, extent, cuts, -0.22, 0.18) * array
    return jnp.clip(array, min=-limit, max=limit).astype(held_as)


def setup_inputs(seed: int = 0) -> dict:
    keys = jax.random.split(jax.random.key(seed), 3)
    field = gaussian(keys[0], (C, NLAT * NLON), 1.0, 6.0, ((0, 8), (1, 64)), jnp.float32)
    mixing = gaussian(keys[1], (MODES, 2, C, C), (10 * (2 * C) ** -0.5), 6.0, ((0, 64), (2, 8)), jnp.float32)
    return dict(field=field, mixing=mixing)


def legendre(cosv, sinv, mvals):
    log_diag = 0.5 * (jnp.log(0.5) + lax.lgamma(mvals + 1.5) - lax.lgamma(jnp.ones_like(mvals) * 1.5) - lax.lgamma(mvals + 1.0))
    pmm = jnp.exp(log_diag[None, :] + mvals[None, :] * jnp.log(sinv)[:, None])
    xcol = cosv[:, None]
    mrow = mvals[None, :]

    def advance(carry, degree):
        prev_one, prev_two = carry
        denom_a = jnp.maximum(degree * degree - mrow * mrow, 1.0)
        coef_a = jnp.sqrt((4.0 * degree * degree - 1.0) / denom_a)
        low = degree - 1.0
        coef_b = jnp.sqrt(jnp.maximum(low * low - mrow * mrow, 0.0) / jnp.maximum(4.0 * low * low - 1.0, 1.0))
        general = coef_a * (xcol * prev_one - coef_b * prev_two)
        first = jnp.sqrt(2.0 * mrow + 3.0) * xcol * prev_one
        value = jnp.where(degree < mrow, 0.0, jnp.where(degree == mrow, pmm, jnp.where(degree == mrow + 1.0, first, general)))
        return ((value, prev_one), value)
    zeros = jnp.zeros_like(pmm)
    degrees = jnp.arange(L).astype(jnp.float32)
    _, stacked = lax.scan(advance, (zeros, zeros), degrees)
    return jnp.transpose(stacked, (1, 2, 0))

def dft_tables():
    modes = jnp.arange(MODES).astype(jnp.int32)
    points = jnp.arange(NLON).astype(jnp.int32)
    phase = modes[:, None] * points[None, :] % NLON
    angle = 2.0 * jnp.pi / NLON * phase.astype(jnp.float32)
    return (jnp.cos(angle), jnp.sin(angle))

def reference(field, mixing):
    high = lax.Precision.HIGHEST
    cos_tab, sin_tab = dft_tables()
    grid_in = field.reshape(C, NLAT, NLON)
    real_part = jnp.einsum('crn,mn->rmc', grid_in, cos_tab, precision=high) / NLON
    imag_part = -jnp.einsum('crn,mn->rmc', grid_in, sin_tab, precision=high) / NLON
    spec = jnp.stack([real_part, imag_part], axis=2)
    rows = jnp.arange(NLAT).astype(jnp.float32)
    theta = jnp.pi * (rows + 0.5) / NLAT
    weights = jnp.pi / NLAT * jnp.sin(theta)
    table = legendre(jnp.cos(theta), jnp.sin(theta), jnp.arange(MODES).astype(jnp.float32))
    weighted = table * weights[:, None, None]
    coeffs = jnp.einsum('rml,rmtc->mltc', weighted, spec, precision=high)
    mix_re = mixing[:, 0]
    mix_im = mixing[:, 1]
    new_re = jnp.einsum('mlc,mdc->mld', coeffs[:, :, 0], mix_re, precision=high) - jnp.einsum('mlc,mdc->mld', coeffs[:, :, 1], mix_im, precision=high)
    new_im = jnp.einsum('mlc,mdc->mld', coeffs[:, :, 0], mix_im, precision=high) + jnp.einsum('mlc,mdc->mld', coeffs[:, :, 1], mix_re, precision=high)
    mixed = jnp.stack([new_re, new_im], axis=2)
    back = jnp.einsum('rml,mltc->rmtc', table, mixed, precision=high)
    factor = jnp.where(jnp.arange(MODES) == 0, 1.0, 2.0).astype(jnp.float32)
    grid = jnp.einsum('rmc,mn->crn', back[:, :, 0] * factor[None, :, None], cos_tab, precision=high) - jnp.einsum('rmc,mn->crn', back[:, :, 1] * factor[None, :, None], sin_tab, precision=high)
    return jax.nn.gelu(grid, approximate=False).reshape(C, NLAT * NLON)
```

```python
import functools

import jax
import jax.numpy as jnp
import ml_dtypes
import numpy as np
from jax import lax
from jax.experimental import pallas as pl
from jax.experimental.pallas import tpu as pltpu
from jax.sharding import PartitionSpec as P
from math import lgamma

NLON = 1440
L = 121
MODES = 128
NLAT = 768
BANDS = 64
CHANS = 8
WIN = 1536
GROUP = 4
GROUPS = 3
SPAN = GROUP * NLON
MESH = pl.DeviceIdType.MESH
F32 = jnp.float32
BF16 = jnp.bfloat16


def split(table):
    high = table.astype(np.float32).astype(ml_dtypes.bfloat16)
    low = (table - high.astype(np.float64)).astype(ml_dtypes.bfloat16)
    return high, low


def dft_tables():
    n = np.arange(NLON)
    col = np.arange(2 * MODES)
    quarter, k = col // 64, col % 64
    m = 2 * k + quarter // 2
    angle = 2.0 * np.pi / NLON * ((n[:, None] * m[None, :]) % NLON)
    wave = np.where(quarter[None, :] % 2 == 0, np.cos(angle), -np.sin(angle))
    forward = np.zeros((WIN, 2 * MODES))
    forward[:NLON] = wave / NLON
    backward = np.zeros((2 * MODES, WIN))
    backward[:, :NLON] = (wave * np.where(m == 0, 1.0, 2.0)[None, :]).T
    return split(forward), split(backward)


def row_constants():
    j = np.arange(NLAT)
    place = j // 256, j % 256 // GROUP, j % GROUP
    row = 12 * place[1] + GROUP * place[0] + place[2]
    theta = np.pi * (row + 0.5) / NLAT
    out = np.zeros((8, NLAT))
    out[0] = np.cos(theta)
    out[1] = np.log(np.sin(theta))
    out[2] = np.pi / NLAT * np.sin(theta)
    diag = [
        0.5 * (np.log(0.5) + lgamma(m + 1.5) - lgamma(1.5) - lgamma(m + 1.0)) for m in range(MODES)
    ]
    return out.astype(np.float32), np.repeat(np.array(diag)[:, None], 128, 1).astype(np.float32)


def halves(value):
    high = value.astype(BF16)
    return high, (value - high.astype(F32)).astype(BF16)


def dot(a, b):
    return jnp.dot(a, b, preferred_element_type=F32)


def lane_mask(rows):
    return lax.broadcasted_iota(jnp.int32, (rows, 128), 1) < 64


def forward_rows(block, fh, fl):
    rows = []
    for s in range(GROUP):
        window = block[:, 1408 * s : 1408 * s + WIN]
        rows.append(window if s == 0 else pltpu.roll(window, WIN - 32 * s, 1))
    high, low = halves(jnp.concatenate(rows, 0))
    both = dot(jnp.concatenate([high, low], 0), fh)
    z = both[:128] + both[128:] + dot(high, fl)
    lt = lane_mask(32)
    out = []
    for p in range(2):
        pieces = []
        for half in range(2):
            z0 = z[64 * p : 64 * p + 32, 128 * half : 128 * half + 128]
            z1 = z[64 * p + 32 : 64 * p + 64, 128 * half : 128 * half + 128]
            pieces.append(jnp.where(lt, z0, pltpu.roll(z1, 64, 1)))
            pieces.append(jnp.where(lt, pltpu.roll(z0, 64, 1), z1))
        v = jnp.concatenate(pieces, 0).T
        out += [v[:64], v[64:]]
    return out


def backward_lhs(quarters):
    lt = lane_mask(32)
    rows = []
    for p in range(2):
        u = jnp.concatenate([quarters[2 * p], quarters[2 * p + 1]], 0).T
        u0, u1, u2, u3 = (u[32 * q : 32 * q + 32] for q in range(4))
        rows.append(
            jnp.concatenate(
                [jnp.where(lt, u0, pltpu.roll(u1, 64, 1)), jnp.where(lt, u2, pltpu.roll(u3, 64, 1))], 1
            )
        )
        rows.append(
            jnp.concatenate(
                [jnp.where(lt, pltpu.roll(u0, 64, 1), u1), jnp.where(lt, pltpu.roll(u2, 64, 1), u3)], 1
            )
        )
    return jnp.concatenate(rows, 0)


def gelu(v):
    return 0.5 * v * (1.0 + lax.erf(v * np.float32(np.sqrt(0.5))))


def legendre_tables(me, rowc, ldt, coef, table, pw, pt):
    for mh in range(2):
        m = 2 * me + mh
        mf = m.astype(F32)
        deg = lax.broadcasted_iota(jnp.int32, (128, 128), 0).astype(F32)
        denom = jnp.maximum(deg * deg - mf * mf, 1.0)
        ca = jnp.sqrt(jnp.maximum(4.0 * deg * deg - 1.0, 0.0) / denom)
        low = deg - 1.0
        cb = jnp.sqrt(jnp.maximum(low * low - mf * mf, 0.0) / jnp.maximum(4.0 * low * low - 1.0, 1.0))
        first = jnp.sqrt(2.0 * mf + 3.0 + jnp.zeros_like(deg))
        coef[3 * mh] = jnp.where(deg > mf + 1.0, ca, jnp.where(deg == mf + 1.0, first, 0.0))
        coef[3 * mh + 1] = jnp.where(deg > mf + 1.0, ca * cb, 0.0)
        coef[3 * mh + 2] = jnp.where(deg == mf, 1.0, 0.0)
    xcol = rowc[0:1, :]
    logsin = rowc[1:2, :]
    wide = lambda ref, mh, l: jnp.concatenate([ref[mh, pl.ds(l, 1), :]] * 6, 1)
    pmm = []
    for mh in range(2):
        m = 2 * me + mh
        diag = jnp.concatenate([ldt[pl.ds(m, 1), :]] * 6, 1)
        pmm.append(jnp.exp(diag + m.astype(F32) * logsin))

    def advance(l, carry):
        out = []
        for mh in range(2):
            one, two = carry[2 * mh], carry[2 * mh + 1]
            value = (
                wide(coef, 3 * mh, l) * xcol * one
                - wide(coef, 3 * mh + 1, l) * two
                + wide(coef, 3 * mh + 2, l) * pmm[mh]
            )
            table[pl.ds(128 * mh + l, 1), :] = value
            out += [value, one]
        return tuple(out)

    zero = xcol * 0.0
    for mh in range(2):
        table[128 * mh + 120 : 128 * mh + 128, :] = jnp.zeros((8, NLAT), F32)
    lax.fori_loop(0, L, advance, (zero,) * 4)

    def lay(g, _):
        part = table[:, pl.ds(pl.multiple_of(256 * g, 256), 256)]
        weight = rowc[2:3, pl.ds(pl.multiple_of(256 * g, 256), 256)]
        high, low = halves(part * weight)
        pw[0, g], pw[1, g] = high, low
        high, low = halves(part.T)
        pt[0, g], pt[1, g] = high, low
        return 0

    lax.fori_loop(0, GROUPS, lay, 0)


def mixing_tables(mixv, wm):
    group = lax.broadcasted_iota(jnp.int32, (32, 128), 1) // 32
    for src in range(CHANS):
        at, g = src // 4, src % 4
        pieces = []
        for mh in range(2):
            re = mixv[mh, 0][:, 128 * at : 128 * at + 128]
            im = mixv[mh, 1][:, 128 * at : 128 * at + 128]
            for a, b in ((re, -im), (im, re)):
                put = lambda v, to: jnp.where(
                    group == to, v if to == g else pltpu.roll(v, 32 * ((to - g) % 4), 1), 0.0
                )
                pieces.append(put(a, 2 * mh) + put(b, 2 * mh + 1))
        high, low = halves(jnp.concatenate(pieces, 0).T)
        wm[128 * src : 128 * src + 128, :] = jnp.concatenate([high, low], 1)


def kernel(
    x_hbm, mix_hbm, fh_hbm, fl_hbm, ih_hbm, il_hbm, rowc, ldt, out_hbm,
    xv, fv, iv, mixv, sent, got, back, home, gath, coef, table, pw, pt, wm, ybuf, yv,
    xsem, fsem, isem, msem, osem, send1, recv1, send2, recv2, gsend, grecv,
):
    me = lax.axis_index("lat")
    ch = lax.axis_index("chan")

    def x_copy(g):
        return pltpu.make_async_copy(
            x_hbm.at[:, pl.ds(pl.multiple_of(SPAN * g, 128), SPAN)], xv.at[g], xsem.at[g]
        )

    def out_copy(g):
        return pltpu.make_async_copy(
            yv.at[g], out_hbm.at[:, pl.ds(pl.multiple_of(SPAN * g, 128), SPAN)], osem.at[g]
        )

    f_copies = [
        pltpu.make_async_copy(h, fv.at[i], fsem.at[i]) for i, h in enumerate((fh_hbm, fl_hbm))
    ]
    i_copies = [
        pltpu.make_async_copy(h, iv.at[i], isem.at[i]) for i, h in enumerate((ih_hbm, il_hbm))
    ]
    m_copy = pltpu.make_async_copy(mix_hbm, mixv, msem)
    f_copies[0].start()
    f_copies[1].start()
    for g in range(GROUPS):
        x_copy(g).start()
    m_copy.start()
    i_copies[0].start()
    i_copies[1].start()

    barrier = pltpu.get_barrier_semaphore()

    def greet_lat(i, _):
        pl.semaphore_signal(
            barrier, inc=1, device_id=(lax.rem(me + i, BANDS), ch), device_id_type=MESH
        )
        return 0

    def greet_chan(i, _):
        pl.semaphore_signal(
            barrier, inc=1, device_id=(me, lax.rem(ch + i, CHANS)), device_id_type=MESH
        )
        return 0

    lax.fori_loop(1, BANDS, greet_lat, 0)
    lax.fori_loop(1, CHANS, greet_chan, 0)
    pl.semaphore_wait(barrier, BANDS - 1 + CHANS - 1)

    def spread(src, dst, send, recv, g):
        def one(i, _):
            peer = lax.rem(me + i, BANDS)
            pltpu.make_async_remote_copy(
                src_ref=src.at[g, pl.ds(pl.multiple_of(4 * peer, 4), 4)],
                dst_ref=dst.at[g, pl.ds(pl.multiple_of(4 * me, 4), 4)],
                send_sem=send.at[g],
                recv_sem=recv.at[g],
                device_id=(peer, ch),
                device_id_type=MESH,
            ).start()
            return 0

        lax.fori_loop(1, BANDS, one, 0)
        own = pl.ds(pl.multiple_of(4 * me, 4), 4)
        pltpu.make_async_copy(src.at[g, own], dst.at[g, own], recv.at[g]).start()

    def arrived(dst, recv, g):
        pltpu.make_async_copy(dst.at[g], dst.at[g], recv.at[g]).wait()

    def gone(src, send, g):
        most = pl.ds(0, 4 * (BANDS - 1))
        pltpu.make_async_copy(src.at[g, most], src.at[g, most], send.at[g]).wait()

    f_copies[0].wait()
    f_copies[1].wait()

    def dft(g, _):
        x_copy(g).wait()
        parts = forward_rows(xv[g], fv[0], fv[1])
        for s in range(GROUP):
            sent[g, pl.ds(s, BANDS, stride=GROUP), :] = parts[s]
        spread(sent, got, send1, recv1, g)
        return 0

    lax.fori_loop(0, GROUPS, dft, 0)

    legendre_tables(me, rowc, ldt, coef, table, pw, pt)
    m_copy.wait()
    mixing_tables(mixv, wm)

    total = jnp.zeros((256, 128), F32)
    for g in range(GROUPS):
        arrived(got, recv1, g)
        high, low = halves(got[g])
        both = dot(pw[0, g], jnp.concatenate([high, low], 1))
        total = total + both[:, :128] + both[:, 128:] + dot(pw[1, g], high)
    lt = lane_mask(128)
    gath[ch] = jnp.where(lt, total[:128], total[128:])

    def gather(i):
        return pltpu.make_async_remote_copy(
            src_ref=gath.at[ch],
            dst_ref=gath.at[ch],
            send_sem=gsend.at[i],
            recv_sem=grecv.at[i],
            device_id=(me, lax.rem(ch + i, CHANS)),
            device_id_type=MESH,
        )

    for i in range(1, CHANS):
        gather(i).start()
    for i in range(1, CHANS):
        gather(i).wait()
    high, low = halves(jnp.concatenate([gath[src] for src in range(CHANS)], 1))
    both = dot(high, wm[...])
    mixed = both[:, :128] + both[:, 128:] + dot(low, wm[:, :128])

    stacked = jnp.concatenate([jnp.where(lt, mixed, 0.0), jnp.where(lt, 0.0, mixed)], 0)
    mhigh, mlow = halves(stacked)
    mboth = jnp.concatenate([mhigh, mlow], 1)
    for g in range(GROUPS):
        both = dot(pt[0, g], mboth)
        back[g] = both[:, :128] + both[:, 128:] + dot(pt[1, g], mhigh)
        spread(back, home, send2, recv2, g)
    i_copies[0].wait()
    i_copies[1].wait()

    def inverse(g, _):
        arrived(home, recv2, g)
        z = backward_lhs([home[g, pl.ds(s, BANDS, stride=GROUP), :] for s in range(GROUP)])
        high, low = halves(z)
        stack = jnp.concatenate([high, low], 0)
        for t in range(WIN // 256):
            cols = slice(256 * t, 256 * t + 256)
            both = dot(stack, iv[0, :, cols])
            ybuf[:, cols] = both[:128] + both[128:] + dot(high, iv[1, :, cols])
        last = None
        lane = lax.broadcasted_iota(jnp.int32, (32, 128), 1)
        for s in range(GROUP):
            row = ybuf[32 * s : 32 * s + 32, :]
            at = 1408 * s
            first = row[:, :128]
            if s > 0:
                row = pltpu.roll(row, 32 * s, 1)
                first = jnp.where(lane < 32 * s, last, row[:, :128])
            last = row[:, 1408:]
            yv[g, :, at : at + 128] = gelu(first)
            yv[g, :, at + 128 : at + 1408] = gelu(row[:, 128:1408])
        yv[g, :, SPAN - 128 :] = gelu(last)
        out_copy(g).start()
        return 0

    lax.fori_loop(0, GROUPS, inverse, 0)
    for g in range(GROUPS):
        gone(sent, send1, g)
        gone(back, send2, g)
        out_copy(g).wait()


def shards(field, mixing):
    (fh, fl), (ih, il) = dft_tables()
    rowc, ldt = row_constants()
    anywhere = pl.BlockSpec(memory_space=pl.ANY)
    inside = pl.BlockSpec(memory_space=pltpu.VMEM)
    dma = pltpu.SemaphoreType.DMA
    exchange = pltpu.VMEM((GROUPS, 4 * BANDS, 128), F32)
    return pl.pallas_call(
        kernel,
        out_shape=jax.ShapeDtypeStruct(field.shape, F32),
        in_specs=[anywhere] * 6 + [inside] * 2,
        out_specs=anywhere,
        scratch_shapes=[
            pltpu.VMEM((GROUPS, 32, SPAN), F32),
            pltpu.VMEM((2, WIN, 256), BF16),
            pltpu.VMEM((2, 256, WIN), BF16),
            pltpu.VMEM((2, 2, 32, 256), F32),
            exchange,
            exchange,
            exchange,
            exchange,
            pltpu.VMEM((CHANS, 128, 128), F32),
            pltpu.VMEM((6, 128, 128), F32),
            pltpu.VMEM((256, NLAT), F32),
            pltpu.VMEM((2, GROUPS, 256, 256), BF16),
            pltpu.VMEM((2, GROUPS, 256, 256), BF16),
            pltpu.VMEM((128 * CHANS, 256), BF16),
            pltpu.VMEM((128, WIN), F32),
            pltpu.VMEM((GROUPS, 32, SPAN), F32),
            dma((GROUPS,)),
            dma((2,)),
            dma((2,)),
            dma,
            dma((GROUPS,)),
            dma((GROUPS,)),
            dma((GROUPS,)),
            dma((GROUPS,)),
            dma((GROUPS,)),
            dma((CHANS,)),
            dma((CHANS,)),
        ],
        compiler_params=pltpu.CompilerParams(
            collective_id=0, has_side_effects=True, vmem_limit_bytes=40 << 20
        ),
        cost_estimate=pl.CostEstimate(flops=2_000_000_000, bytes_accessed=8_000_000, transcendentals=600_000),
    )(
        field,
        mixing,
        jnp.asarray(fh),
        jnp.asarray(fl),
        jnp.asarray(ih),
        jnp.asarray(il),
        jnp.asarray(rowc),
        jnp.asarray(ldt),
    )


def solution(mesh):
    placed = (P("chan", "lat"), P("lat", None, "chan", None))
    return jax.shard_map(
        shards, mesh=mesh, in_specs=placed, out_specs=P("chan", "lat"), check_vma=False
    )
```

```python
import functools

import jax
import jax.numpy as jnp
import ml_dtypes
import numpy as np
from jax import lax
from jax.experimental import pallas as pl
from jax.experimental.pallas import tpu as pltpu
from jax.sharding import PartitionSpec as P
from math import lgamma

NLON = 1440
L = 121
MODES = 128
NLAT = 768
BANDS = 64
CHANS = 8
WIN = 1536
GROUP = 4
GROUPS = 3
SPAN = GROUP * NLON
PAIRS = NLAT // 2
OWN = 6
MESH = pl.DeviceIdType.MESH
F32 = jnp.float32
BF16 = jnp.bfloat16


def split(table):
    high = table.astype(np.float32).astype(ml_dtypes.bfloat16)
    low = (table - high.astype(np.float64)).astype(ml_dtypes.bfloat16)
    return high, low


def dft_tables():
    n = np.arange(NLON)
    col = np.arange(2 * MODES)
    quarter, k = col // 64, col % 64
    m = 2 * k + quarter // 2
    angle = 2.0 * np.pi / NLON * ((n[:, None] * m[None, :]) % NLON)
    wave = np.where(quarter[None, :] % 2 == 0, np.cos(angle), -np.sin(angle))
    forward = np.zeros((WIN, 2 * MODES))
    forward[:NLON] = wave / NLON
    backward = np.zeros((2 * MODES, WIN))
    backward[:, :NLON] = (wave * np.where(m == 0, 1.0, 2.0)[None, :]).T
    return split(forward), split(backward)


def row_constants():
    j = np.arange(NLAT)
    row = 2 * (j % PAIRS) + j // PAIRS
    theta = np.pi * (row + 0.5) / NLAT
    out = np.zeros((8, NLAT))
    out[0] = np.cos(theta)
    out[1] = np.log(np.sin(theta))
    out[2] = np.pi / NLAT * np.sin(theta)
    diag = [
        0.5 * (np.log(0.5) + lgamma(m + 1.5) - lgamma(1.5) - lgamma(m + 1.0)) for m in range(MODES)
    ]
    return out.astype(np.float32), np.repeat(np.array(diag)[:, None], 128, 1).astype(np.float32)


def halves(value):
    high = value.astype(BF16)
    return high, (value - high.astype(F32)).astype(BF16)


def dot(a, b):
    return jnp.dot(a, b, preferred_element_type=F32)


def lane_mask(rows):
    return lax.broadcasted_iota(jnp.int32, (rows, 128), 1) < 64


def forward_rows(block, fh, fl):
    rows = []
    for s in range(GROUP):
        window = block[:, 1408 * s : 1408 * s + WIN]
        rows.append(window if s == 0 else pltpu.roll(window, WIN - 32 * s, 1))
    high, low = halves(jnp.concatenate(rows, 0))
    both = dot(jnp.concatenate([high, low], 0), fh)
    z = both[:128] + both[128:] + dot(high, fl)
    lt = lane_mask(32)
    out = []
    for mh in range(2):
        pieces = []
        for jj in range(2):
            z0 = z[32 * jj : 32 * jj + 32, 128 * mh : 128 * mh + 128]
            z1 = z[64 + 32 * jj : 96 + 32 * jj, 128 * mh : 128 * mh + 128]
            pieces.append(jnp.where(lt, z0, pltpu.roll(z1, 64, 1)))
            pieces.append(jnp.where(lt, pltpu.roll(z0, 64, 1), z1))
        out.append(jnp.concatenate(pieces, 0).T)
    return out


def backward_lhs(v):
    lt = lane_mask(32)
    rows = [[], [], [], []]
    for mh in range(2):
        u = v[mh].T
        for jj in range(2):
            u0 = u[64 * jj : 64 * jj + 32]
            u1 = u[64 * jj + 32 : 64 * jj + 64]
            rows[jj].append(jnp.where(lt, u0, pltpu.roll(u1, 64, 1)))
            rows[2 + jj].append(jnp.where(lt, pltpu.roll(u0, 64, 1), u1))
    return jnp.concatenate([jnp.concatenate(r, 1) for r in rows], 0)


def gelu(v):
    return 0.5 * v * (1.0 + lax.erf(v * np.float32(np.sqrt(0.5))))


def legendre_tables(me, rowc, ldt, coef, table, pw, pt):
    for mh in range(2):
        m = 2 * me + mh
        mf = m.astype(F32)
        deg = lax.broadcasted_iota(jnp.int32, (128, 128), 0).astype(F32)
        denom = jnp.maximum(deg * deg - mf * mf, 1.0)
        ca = jnp.sqrt(jnp.maximum(4.0 * deg * deg - 1.0, 0.0) / denom)
        low = deg - 1.0
        cb = jnp.sqrt(jnp.maximum(low * low - mf * mf, 0.0) / jnp.maximum(4.0 * low * low - 1.0, 1.0))
        first = jnp.sqrt(2.0 * mf + 3.0 + jnp.zeros_like(deg))
        coef[3 * mh] = jnp.where(deg > mf + 1.0, ca, jnp.where(deg == mf + 1.0, first, 0.0))
        coef[3 * mh + 1] = jnp.where(deg > mf + 1.0, ca * cb, 0.0)
        coef[3 * mh + 2] = jnp.where(deg == mf, 1.0, 0.0)
    xcol = rowc[0:1, :]
    logsin = rowc[1:2, :]
    wide = lambda ref, mh, l: jnp.concatenate([ref[mh, pl.ds(l, 1), :]] * 6, 1)
    pmm = []
    for mh in range(2):
        m = 2 * me + mh
        diag = jnp.concatenate([ldt[pl.ds(m, 1), :]] * 6, 1)
        pmm.append(jnp.exp(diag + m.astype(F32) * logsin))

    def advance(l, carry):
        out = []
        for mh in range(2):
            one, two = carry[2 * mh], carry[2 * mh + 1]
            value = (
                wide(coef, 3 * mh, l) * xcol * one
                - wide(coef, 3 * mh + 1, l) * two
                + wide(coef, 3 * mh + 2, l) * pmm[mh]
            )
            table[pl.ds(128 * mh + l, 1), :] = value
            out += [value, one]
        return tuple(out)

    zero = xcol * 0.0
    for mh in range(2):
        table[128 * mh + 120 : 128 * mh + 128, :] = jnp.zeros((8, NLAT), F32)
    lax.fori_loop(0, L, advance, (zero,) * 4)

    for mh in range(2):
        for jj in range(2):
            part = table[128 * mh : 128 * mh + 128, PAIRS * jj : PAIRS * jj + PAIRS]
            high, low = halves(part * rowc[2:3, PAIRS * jj : PAIRS * jj + PAIRS])
            at = slice(128 * jj, 128 * jj + 128)
            pw[0, mh, at], pw[1, mh, at] = high, low
            high, low = halves(part.T)
            pt[0, mh, :, at], pt[1, mh, :, at] = high, low


def mixing_tables(mixv, wm):
    group = lax.broadcasted_iota(jnp.int32, (32, 128), 1) // 32
    for mh in range(2):
        for src in range(CHANS):
            at, g = src // 4, src % 4
            re = mixv[mh, 0][:, 128 * at : 128 * at + 128]
            im = mixv[mh, 1][:, 128 * at : 128 * at + 128]
            pieces = []
            for lh in range(2):
                for a, b in ((re, -im), (im, re)):
                    put = lambda v, to: jnp.where(
                        group == to, v if to == g else pltpu.roll(v, 32 * ((to - g) % 4), 1), 0.0
                    )
                    pieces.append(put(a, 2 * lh) + put(b, 2 * lh + 1))
            high, low = halves(jnp.concatenate(pieces, 0).T)
            wm[mh, 128 * src : 128 * src + 128, :] = jnp.concatenate([high, low], 1)


def kernel(
    x_hbm, mix_hbm, fh_hbm, fl_hbm, ih_hbm, il_hbm, rowc_hbm, ldt_hbm, out_hbm,
    rowc, ldt, xv, fv, iv, mixv, sent, got, back, home, gath, coef, table, pw, pt, wm, ybuf, yv,
    csem, xsem, fsem, isem, msem, osem, send1, recv1, send2, recv2, gsend, grecv,
):
    me = lax.axis_index("lat")
    ch = lax.axis_index("chan")

    def x_copy(g):
        return pltpu.make_async_copy(
            x_hbm.at[:, pl.ds(pl.multiple_of(SPAN * g, 128), SPAN)], xv.at[g], xsem.at[g]
        )

    def out_copy(g):
        return pltpu.make_async_copy(
            yv.at[g], out_hbm.at[:, pl.ds(pl.multiple_of(SPAN * g, 128), SPAN)], osem.at[g]
        )

    f_copies = [
        pltpu.make_async_copy(h, fv.at[i], fsem.at[i]) for i, h in enumerate((fh_hbm, fl_hbm))
    ]
    i_copies = [
        pltpu.make_async_copy(h, iv.at[i], isem.at[i]) for i, h in enumerate((ih_hbm, il_hbm))
    ]
    m_copy = pltpu.make_async_copy(mix_hbm, mixv, msem)
    f_copies[0].start()
    f_copies[1].start()
    for g in range(GROUPS):
        x_copy(g).start()
    m_copy.start()
    c_copies = [
        pltpu.make_async_copy(rowc_hbm, rowc, csem.at[0]),
        pltpu.make_async_copy(ldt_hbm, ldt, csem.at[1]),
    ]
    c_copies[0].start()
    c_copies[1].start()
    i_copies[0].start()
    i_copies[1].start()

    barrier = pltpu.get_barrier_semaphore()

    def greet_lat(i, _):
        pl.semaphore_signal(
            barrier, inc=1, device_id=(lax.rem(me + i, BANDS), ch), device_id_type=MESH
        )
        return 0

    def greet_chan(i, _):
        pl.semaphore_signal(
            barrier, inc=1, device_id=(me, lax.rem(ch + i, CHANS)), device_id_type=MESH
        )
        return 0

    lax.fori_loop(1, BANDS, greet_lat, 0)
    lax.fori_loop(1, CHANS, greet_chan, 0)
    pl.semaphore_wait(barrier, BANDS - 1 + CHANS - 1)

    def spread(src, dst, send, recv, mh):
        def one(i, _):
            peer = lax.rem(me + i, BANDS)
            pltpu.make_async_remote_copy(
                src_ref=src.at[mh, pl.ds(OWN * peer, OWN)],
                dst_ref=dst.at[mh, pl.ds(OWN * me, OWN)],
                send_sem=send.at[mh],
                recv_sem=recv.at[mh],
                device_id=(peer, ch),
                device_id_type=MESH,
            ).start()
            return 0

        lax.fori_loop(1, BANDS, one, 0)
        own = pl.ds(OWN * me, OWN)
        pltpu.make_async_copy(src.at[mh, own], dst.at[mh, own], recv.at[mh]).start()

    def arrived(dst, recv, mh):
        pltpu.make_async_copy(dst.at[mh], dst.at[mh], recv.at[mh]).wait()

    def gone(src, send, mh):
        most = pl.ds(0, OWN * (BANDS - 1))
        pltpu.make_async_copy(src.at[mh, most], src.at[mh, most], send.at[mh]).wait()

    f_copies[0].wait()
    f_copies[1].wait()

    def dft(g, _):
        x_copy(g).wait()
        parts = forward_rows(xv[g], fv[0], fv[1])
        for mh in range(2):
            for p in range(2):
                sent[mh, pl.ds(2 * g + p, BANDS, stride=OWN), :] = parts[mh][64 * p : 64 * p + 64]
        return 0

    lax.fori_loop(0, GROUPS, dft, 0)
    for mh in range(2):
        spread(sent, got, send1, recv1, mh)

    c_copies[0].wait()
    c_copies[1].wait()
    legendre_tables(me, rowc, ldt, coef, table, pw, pt)
    m_copy.wait()
    mixing_tables(mixv, wm)

    def gather(mh, i):
        return pltpu.make_async_remote_copy(
            src_ref=gath.at[mh, ch],
            dst_ref=gath.at[mh, ch],
            send_sem=gsend.at[mh, i],
            recv_sem=grecv.at[mh, i],
            device_id=(me, lax.rem(ch + i, CHANS)),
            device_id_type=MESH,
        )

    lt = lane_mask(128)
    lt64 = lane_mask(64)
    for mh in range(2):
        arrived(got, recv1, mh)
        high, low = halves(got[mh])
        both = dot(pw[0, mh], jnp.concatenate([high, low], 1))
        total = both[:, :128] + both[:, 128:] + dot(pw[1, mh], high)
        both = jnp.where(lt, total[:128], total[128:])
        both = both + pltpu.roll(both, 64, 1)
        gath[mh, ch] = jnp.where(lt64, both[:64], both[64:])
        for i in range(1, CHANS):
            gather(mh, i).start()

    for mh in range(2):
        for i in range(1, CHANS):
            gather(mh, i).wait()
        high, low = halves(jnp.concatenate([gath[mh, src] for src in range(CHANS)], 1))
        both = dot(high, wm[mh])
        mixed = both[:, :128] + both[:, 128:] + dot(low, wm[mh, :, :128])
        turned = pltpu.roll(mixed, 64, 1)
        stacked = jnp.concatenate(
            [
                jnp.where(lt64, mixed, 0.0),
                jnp.where(lt64, turned, 0.0),
                jnp.where(lt64, 0.0, turned),
                jnp.where(lt64, 0.0, mixed),
            ],
            0,
        )
        mhigh, mlow = halves(stacked)
        both = dot(pt[0, mh], jnp.concatenate([mhigh, mlow], 1))
        back[mh] = both[:, :128] + both[:, 128:] + dot(pt[1, mh], mhigh)
        spread(back, home, send2, recv2, mh)
    i_copies[0].wait()
    i_copies[1].wait()
    for mh in range(2):
        arrived(home, recv2, mh)

    def inverse(g, _):
        v = [
            jnp.concatenate([home[mh, pl.ds(2 * g + p, BANDS, stride=OWN), :] for p in range(2)], 0)
            for mh in range(2)
        ]
        z = backward_lhs(v)
        high, low = halves(z)
        stack = jnp.concatenate([high, low], 0)
        for t in range(WIN // 256):
            cols = slice(256 * t, 256 * t + 256)
            both = dot(stack, iv[0, :, cols])
            ybuf[:, cols] = both[:128] + both[128:] + dot(high, iv[1, :, cols])
        last = None
        lane = lax.broadcasted_iota(jnp.int32, (32, 128), 1)
        for s in range(GROUP):
            row = ybuf[32 * s : 32 * s + 32, :]
            at = 1408 * s
            first = row[:, :128]
            if s > 0:
                row = pltpu.roll(row, 32 * s, 1)
                first = jnp.where(lane < 32 * s, last, row[:, :128])
            last = row[:, 1408:]
            yv[g, :, at : at + 128] = gelu(first)
            yv[g, :, at + 128 : at + 1408] = gelu(row[:, 128:1408])
        yv[g, :, SPAN - 128 :] = gelu(last)
        out_copy(g).start()
        return 0

    lax.fori_loop(0, GROUPS, inverse, 0)
    for g in range(GROUPS):
        out_copy(g).wait()
    for mh in range(2):
        gone(sent, send1, mh)
        gone(back, send2, mh)


def shards(field, mixing):
    (fh, fl), (ih, il) = dft_tables()
    rowc, ldt = row_constants()
    anywhere = pl.BlockSpec(memory_space=pltpu.HBM)
    dma = pltpu.SemaphoreType.DMA
    exchange = pltpu.VMEM((2, PAIRS, 128), F32)
    return pl.pallas_call(
        kernel,
        out_shape=jax.ShapeDtypeStruct(field.shape, F32),
        in_specs=[anywhere] * 8,
        out_specs=anywhere,
        scratch_shapes=[
            pltpu.VMEM((8, NLAT), F32),
            pltpu.VMEM((MODES, 128), F32),
            pltpu.VMEM((GROUPS, 32, SPAN), F32),
            pltpu.VMEM((2, WIN, 256), BF16),
            pltpu.VMEM((2, 256, WIN), BF16),
            pltpu.VMEM((2, 2, 32, 256), F32),
            exchange,
            exchange,
            exchange,
            exchange,
            pltpu.VMEM((2, CHANS, 64, 128), F32),
            pltpu.VMEM((6, 128, 128), F32),
            pltpu.VMEM((256, NLAT), F32),
            pltpu.VMEM((2, 2, 256, PAIRS), BF16),
            pltpu.VMEM((2, 2, PAIRS, 256), BF16),
            pltpu.VMEM((2, 128 * CHANS, 256), BF16),
            pltpu.VMEM((128, WIN), F32),
            pltpu.VMEM((GROUPS, 32, SPAN), F32),
            dma((2,)),
            dma((GROUPS,)),
            dma((2,)),
            dma((2,)),
            dma,
            dma((GROUPS,)),
            dma((2,)),
            dma((2,)),
            dma((2,)),
            dma((2,)),
            dma((2, CHANS)),
            dma((2, CHANS)),
        ],
        compiler_params=pltpu.CompilerParams(
            collective_id=0, has_side_effects=True, vmem_limit_bytes=60 << 20
        ),
        cost_estimate=pl.CostEstimate(flops=2_000_000_000, bytes_accessed=8_000_000, transcendentals=600_000),
    )(
        field,
        mixing,
        jnp.asarray(fh),
        jnp.asarray(fl),
        jnp.asarray(ih),
        jnp.asarray(il),
        jnp.asarray(rowc),
        jnp.asarray(ldt),
    )


def solution(mesh):
    placed = (P("chan", "lat"), P("lat", None, "chan", None))
    return jax.shard_map(
        shards, mesh=mesh, in_specs=placed, out_specs=P("chan", "lat"), check_vma=False
    )
```

```python
import functools

import jax
import jax.numpy as jnp
import ml_dtypes
import numpy as np
from jax import lax
from jax.experimental import pallas as pl
from jax.experimental.pallas import tpu as pltpu
from jax.sharding import PartitionSpec as P
from math import lgamma

NLON = 1440
L = 121
MODES = 128
NLAT = 768
BANDS = 64
CHANS = 8
WIN = 1536
GROUP = 4
GROUPS = 3
SPAN = GROUP * NLON
PAIRS = NLAT // 2
OWN = 6
MESH = pl.DeviceIdType.MESH
F32 = jnp.float32
BF16 = jnp.bfloat16


def split(table):
    high = table.astype(np.float32).astype(ml_dtypes.bfloat16)
    low = (table - high.astype(np.float64)).astype(ml_dtypes.bfloat16)
    return high, low


def dft_tables():
    n = np.arange(NLON)
    col = np.arange(2 * MODES)
    quarter, k = col // 64, col % 64
    m = 2 * k + quarter // 2
    angle = 2.0 * np.pi / NLON * ((n[:, None] * m[None, :]) % NLON)
    wave = np.where(quarter[None, :] % 2 == 0, np.cos(angle), -np.sin(angle))
    forward = np.zeros((WIN, 2 * MODES))
    forward[:NLON] = wave / NLON
    backward = np.zeros((2 * MODES, WIN))
    backward[:, :NLON] = (wave * np.where(m == 0, 1.0, 2.0)[None, :]).T
    return split(forward), split(backward)


def row_constants():
    j = np.arange(NLAT)
    row = 2 * (j % PAIRS) + j // PAIRS
    theta = np.pi * (row + 0.5) / NLAT
    out = np.zeros((8, NLAT))
    out[0] = np.cos(theta)
    out[1] = np.log(np.sin(theta))
    out[2] = np.pi / NLAT * np.sin(theta)
    diag = [
        0.5 * (np.log(0.5) + lgamma(m + 1.5) - lgamma(1.5) - lgamma(m + 1.0)) for m in range(MODES)
    ]
    return out.astype(np.float32), np.repeat(np.array(diag)[:, None], 128, 1).astype(np.float32)


def halves(value):
    high = value.astype(BF16)
    return high, (value - high.astype(F32)).astype(BF16)


def dot(a, b):
    return jnp.dot(a, b, preferred_element_type=F32)


def lane_mask(rows):
    return lax.broadcasted_iota(jnp.int32, (rows, 128), 1) < 64


def forward_rows(block, fh, fl):
    rows = []
    for s in range(GROUP):
        window = block[:, 1408 * s : 1408 * s + WIN]
        rows.append(window if s == 0 else pltpu.roll(window, WIN - 32 * s, 1))
    high, low = halves(jnp.concatenate(rows, 0))
    both = dot(jnp.concatenate([high, low], 0), fh)
    z = both[:128] + both[128:] + dot(high, fl)
    lt = lane_mask(32)
    out = []
    for mh in range(2):
        pieces = []
        for jj in range(2):
            z0 = z[32 * jj : 32 * jj + 32, 128 * mh : 128 * mh + 128]
            z1 = z[64 + 32 * jj : 96 + 32 * jj, 128 * mh : 128 * mh + 128]
            pieces.append(jnp.where(lt, z0, pltpu.roll(z1, 64, 1)))
            pieces.append(jnp.where(lt, pltpu.roll(z0, 64, 1), z1))
        out.append(jnp.concatenate(pieces, 0).T)
    return out


def backward_lhs(v):
    lt = lane_mask(32)
    rows = [[], [], [], []]
    for mh in range(2):
        u = v[mh].T
        for jj in range(2):
            u0 = u[64 * jj : 64 * jj + 32]
            u1 = u[64 * jj + 32 : 64 * jj + 64]
            rows[jj].append(jnp.where(lt, u0, pltpu.roll(u1, 64, 1)))
            rows[2 + jj].append(jnp.where(lt, pltpu.roll(u0, 64, 1), u1))
    return jnp.concatenate([jnp.concatenate(r, 1) for r in rows], 0)


def gelu(v):
    return 0.5 * v * (1.0 + lax.erf(v * np.float32(np.sqrt(0.5))))


def legendre_tables(me, rowc, ldt, coef, table, pw, pt):
    for mh in range(2):
        m = 2 * me + mh
        mf = m.astype(F32)
        deg = lax.broadcasted_iota(jnp.int32, (128, 128), 0).astype(F32)
        denom = jnp.maximum(deg * deg - mf * mf, 1.0)
        ca = jnp.sqrt(jnp.maximum(4.0 * deg * deg - 1.0, 0.0) / denom)
        low = deg - 1.0
        cb = jnp.sqrt(jnp.maximum(low * low - mf * mf, 0.0) / jnp.maximum(4.0 * low * low - 1.0, 1.0))
        first = jnp.sqrt(2.0 * mf + 3.0 + jnp.zeros_like(deg))
        coef[3 * mh] = jnp.where(deg > mf + 1.0, ca, jnp.where(deg == mf + 1.0, first, 0.0))
        coef[3 * mh + 1] = jnp.where(deg > mf + 1.0, ca * cb, 0.0)
        coef[3 * mh + 2] = jnp.where(deg == mf, 1.0, 0.0)
    xcol = rowc[0:1, :]
    logsin = rowc[1:2, :]
    wide = lambda ref, mh, l: jnp.concatenate([ref[mh, pl.ds(l, 1), :]] * 6, 1)
    pmm = []
    for mh in range(2):
        m = 2 * me + mh
        diag = jnp.concatenate([ldt[pl.ds(m, 1), :]] * 6, 1)
        pmm.append(jnp.exp(diag + m.astype(F32) * logsin))

    def advance(l, carry):
        out = []
        for mh in range(2):
            one, two = carry[2 * mh], carry[2 * mh + 1]
            value = (
                wide(coef, 3 * mh, l) * xcol * one
                - wide(coef, 3 * mh + 1, l) * two
                + wide(coef, 3 * mh + 2, l) * pmm[mh]
            )
            table[pl.ds(128 * mh + l, 1), :] = value
            out += [value, one]
        return tuple(out)

    zero = xcol * 0.0
    for mh in range(2):
        table[128 * mh + 120 : 128 * mh + 128, :] = jnp.zeros((8, NLAT), F32)
    lax.fori_loop(0, L, advance, (zero,) * 4)

    for mh in range(2):
        for jj in range(2):
            part = table[128 * mh : 128 * mh + 128, PAIRS * jj : PAIRS * jj + PAIRS]
            high, low = halves(part * rowc[2:3, PAIRS * jj : PAIRS * jj + PAIRS])
            at = slice(128 * jj, 128 * jj + 128)
            pw[0, mh, at], pw[1, mh, at] = high, low
            high, low = halves(part.T)
            pt[0, mh, :, at], pt[1, mh, :, at] = high, low


def mixing_tables(mixv, wm):
    group = lax.broadcasted_iota(jnp.int32, (32, 128), 1) // 32
    for mh in range(2):
        for src in range(CHANS):
            at, g = src // 4, src % 4
            re = mixv[mh, 0][:, 128 * at : 128 * at + 128]
            im = mixv[mh, 1][:, 128 * at : 128 * at + 128]
            pieces = []
            for lh in range(2):
                for a, b in ((re, -im), (im, re)):
                    put = lambda v, to: jnp.where(
                        group == to, v if to == g else pltpu.roll(v, 32 * ((to - g) % 4), 1), 0.0
                    )
                    pieces.append(put(a, 2 * lh) + put(b, 2 * lh + 1))
            high, low = halves(jnp.concatenate(pieces, 0).T)
            wm[mh, 128 * src : 128 * src + 128, :] = jnp.concatenate([high, low], 1)


def kernel(
    x_hbm, mix_hbm, fh_hbm, fl_hbm, ih_hbm, il_hbm, rowc_hbm, ldt_hbm, out_hbm,
    rowc, ldt, xv, fv, iv, mixv, sent, got, back, home, gath, coef, table, pw, pt, wm, ybuf, yv,
    csem, xsem, fsem, isem, msem, osem, send1, recv1, send2, recv2, gsend, grecv,
):
    me = lax.axis_index("lat")
    ch = lax.axis_index("chan")

    barrier = pltpu.get_barrier_semaphore()

    def far_first(i):
        turn = lambda r: jnp.where(lax.rem(r, 2) == 1, 4 - (r + 1) // 2, 4 + r // 2)
        z = lax.rem(me // 8 + turn(i // 8), 8)
        y = lax.rem(lax.rem(me, 8) + turn(lax.rem(i, 8)), 8)
        return z * 8 + y

    def greet_lat(i, _):
        pl.semaphore_signal(barrier, inc=1, device_id=(far_first(i), ch), device_id_type=MESH)
        return 0

    def greet_chan(i, _):
        pl.semaphore_signal(
            barrier, inc=1, device_id=(me, lax.rem(ch + i, CHANS)), device_id_type=MESH
        )
        return 0

    lax.fori_loop(0, BANDS - 1, greet_lat, 0)
    lax.fori_loop(1, CHANS, greet_chan, 0)

    def x_copy(g):
        return pltpu.make_async_copy(
            x_hbm.at[:, pl.ds(pl.multiple_of(SPAN * g, 128), SPAN)], xv.at[g], xsem.at[g]
        )

    def out_copy(g):
        return pltpu.make_async_copy(
            yv.at[g], out_hbm.at[:, pl.ds(pl.multiple_of(SPAN * g, 128), SPAN)], osem.at[g]
        )

    f_copies = [
        pltpu.make_async_copy(h, fv.at[i], fsem.at[i]) for i, h in enumerate((fh_hbm, fl_hbm))
    ]
    i_copies = [
        pltpu.make_async_copy(h, iv.at[i], isem.at[i]) for i, h in enumerate((ih_hbm, il_hbm))
    ]
    m_copy = pltpu.make_async_copy(mix_hbm, mixv, msem)
    f_copies[0].start()
    f_copies[1].start()
    for g in range(GROUPS):
        x_copy(g).start()
    m_copy.start()
    c_copies = [
        pltpu.make_async_copy(rowc_hbm, rowc, csem.at[0]),
        pltpu.make_async_copy(ldt_hbm, ldt, csem.at[1]),
    ]
    c_copies[0].start()
    c_copies[1].start()
    i_copies[0].start()
    i_copies[1].start()


    def spread(src, dst, send, recv, mh):
        def one(i, _):
            peer = far_first(i)
            pltpu.make_async_remote_copy(
                src_ref=src.at[mh, pl.ds(OWN * peer, OWN)],
                dst_ref=dst.at[mh, pl.ds(OWN * me, OWN)],
                send_sem=send.at[mh],
                recv_sem=recv.at[mh],
                device_id=(peer, ch),
                device_id_type=MESH,
            ).start()
            return 0

        lax.fori_loop(0, BANDS - 1, one, 0)
        own = pl.ds(OWN * me, OWN)
        pltpu.make_async_copy(src.at[mh, own], dst.at[mh, own], recv.at[mh]).start()

    def arrived(dst, recv, mh):
        pltpu.make_async_copy(dst.at[mh], dst.at[mh], recv.at[mh]).wait()

    def gone(src, send, mh):
        most = pl.ds(0, OWN * (BANDS - 1))
        pltpu.make_async_copy(src.at[mh, most], src.at[mh, most], send.at[mh]).wait()

    f_copies[0].wait()
    f_copies[1].wait()

    def dft(g, _):
        x_copy(g).wait()
        parts = forward_rows(xv[g], fv[0], fv[1])
        for mh in range(2):
            for p in range(2):
                sent[mh, pl.ds(2 * g + p, BANDS, stride=OWN), :] = parts[mh][64 * p : 64 * p + 64]
        return 0

    lax.fori_loop(0, GROUPS, dft, 0)
    pl.semaphore_wait(barrier, BANDS - 1 + CHANS - 1)
    for mh in range(2):
        spread(sent, got, send1, recv1, mh)

    c_copies[0].wait()
    c_copies[1].wait()
    legendre_tables(me, rowc, ldt, coef, table, pw, pt)
    m_copy.wait()
    mixing_tables(mixv, wm)

    def gather(mh, i):
        return pltpu.make_async_remote_copy(
            src_ref=gath.at[mh, ch],
            dst_ref=gath.at[mh, ch],
            send_sem=gsend.at[mh, i],
            recv_sem=grecv.at[mh, i],
            device_id=(me, lax.rem(ch + i, CHANS)),
            device_id_type=MESH,
        )

    lt = lane_mask(128)
    lt64 = lane_mask(64)
    for mh in range(2):
        arrived(got, recv1, mh)
        high, low = halves(got[mh])
        both = dot(pw[0, mh], jnp.concatenate([high, low], 1))
        total = both[:, :128] + both[:, 128:] + dot(pw[1, mh], high)
        both = jnp.where(lt, total[:128], total[128:])
        both = both + pltpu.roll(both, 64, 1)
        gath[mh, ch] = jnp.where(lt64, both[:64], both[64:])
        for i in range(1, CHANS):
            gather(mh, i).start()

    for mh in range(2):
        for i in range(1, CHANS):
            gather(mh, i).wait_recv()
        high, low = halves(jnp.concatenate([gath[mh, src] for src in range(CHANS)], 1))
        both = dot(high, wm[mh])
        mixed = both[:, :128] + both[:, 128:] + dot(low, wm[mh, :, :128])
        turned = pltpu.roll(mixed, 64, 1)
        stacked = jnp.concatenate(
            [
                jnp.where(lt64, mixed, 0.0),
                jnp.where(lt64, turned, 0.0),
                jnp.where(lt64, 0.0, turned),
                jnp.where(lt64, 0.0, mixed),
            ],
            0,
        )
        mhigh, mlow = halves(stacked)
        both = dot(pt[0, mh], jnp.concatenate([mhigh, mlow], 1))
        back[mh] = both[:, :128] + both[:, 128:] + dot(pt[1, mh], mhigh)
        spread(back, home, send2, recv2, mh)
    i_copies[0].wait()
    i_copies[1].wait()
    for mh in range(2):
        arrived(home, recv2, mh)

    def inverse(g, _):
        v = [
            jnp.concatenate([home[mh, pl.ds(2 * g + p, BANDS, stride=OWN), :] for p in range(2)], 0)
            for mh in range(2)
        ]
        z = backward_lhs(v)
        high, low = halves(z)
        stack = jnp.concatenate([high, low], 0)
        for t in range(WIN // 256):
            cols = slice(256 * t, 256 * t + 256)
            both = dot(stack, iv[0, :, cols])
            ybuf[:, cols] = both[:128] + both[128:] + dot(high, iv[1, :, cols])
        last = None
        lane = lax.broadcasted_iota(jnp.int32, (32, 128), 1)
        for s in range(GROUP):
            row = ybuf[32 * s : 32 * s + 32, :]
            at = 1408 * s
            first = row[:, :128]
            if s > 0:
                row = pltpu.roll(row, 32 * s, 1)
                first = jnp.where(lane < 32 * s, last, row[:, :128])
            last = row[:, 1408:]
            yv[g, :, at : at + 128] = gelu(first)
            yv[g, :, at + 128 : at + 1408] = gelu(row[:, 128:1408])
        yv[g, :, SPAN - 128 :] = gelu(last)
        out_copy(g).start()
        return 0

    lax.fori_loop(0, GROUPS, inverse, 0)
    for g in range(GROUPS):
        out_copy(g).wait()
    for mh in range(2):
        gone(sent, send1, mh)
        gone(back, send2, mh)
        for i in range(1, CHANS):
            gather(mh, i).wait_send()


def shards(field, mixing):
    (fh, fl), (ih, il) = dft_tables()
    rowc, ldt = row_constants()
    anywhere = pl.BlockSpec(memory_space=pltpu.HBM)
    dma = pltpu.SemaphoreType.DMA
    exchange = pltpu.VMEM((2, PAIRS, 128), F32)
    return pl.pallas_call(
        kernel,
        out_shape=jax.ShapeDtypeStruct(field.shape, F32),
        in_specs=[anywhere] * 8,
        out_specs=anywhere,
        scratch_shapes=[
            pltpu.VMEM((8, NLAT), F32),
            pltpu.VMEM((MODES, 128), F32),
            pltpu.VMEM((GROUPS, 32, SPAN), F32),
            pltpu.VMEM((2, WIN, 256), BF16),
            pltpu.VMEM((2, 256, WIN), BF16),
            pltpu.VMEM((2, 2, 32, 256), F32),
            exchange,
            exchange,
            exchange,
            exchange,
            pltpu.VMEM((2, CHANS, 64, 128), F32),
            pltpu.VMEM((6, 128, 128), F32),
            pltpu.VMEM((256, NLAT), F32),
            pltpu.VMEM((2, 2, 256, PAIRS), BF16),
            pltpu.VMEM((2, 2, PAIRS, 256), BF16),
            pltpu.VMEM((2, 128 * CHANS, 256), BF16),
            pltpu.VMEM((128, WIN), F32),
            pltpu.VMEM((GROUPS, 32, SPAN), F32),
            dma((2,)),
            dma((GROUPS,)),
            dma((2,)),
            dma((2,)),
            dma,
            dma((GROUPS,)),
            dma((2,)),
            dma((2,)),
            dma((2,)),
            dma((2,)),
            dma((2, CHANS)),
            dma((2, CHANS)),
        ],
        compiler_params=pltpu.CompilerParams(
            collective_id=0, has_side_effects=True, vmem_limit_bytes=60 << 20
        ),
        cost_estimate=pl.CostEstimate(flops=2_000_000_000, bytes_accessed=8_000_000, transcendentals=600_000),
    )(
        field,
        mixing,
        jnp.asarray(fh),
        jnp.asarray(fl),
        jnp.asarray(ih),
        jnp.asarray(il),
        jnp.asarray(rowc),
        jnp.asarray(ldt),
    )


def solution(mesh):
    placed = (P("chan", "lat"), P("lat", None, "chan", None))
    return jax.shard_map(
        shards, mesh=mesh, in_specs=placed, out_specs=P("chan", "lat"), check_vma=False
    )
```
